32 devices in a mesh: ctx: 8 (over y, x, core), head: 4 (over z).
Axes of the slice: x: 2, y: 2, z: 4, core: 2. Of those that a mesh axis runs over, the one named last changes fastest.
Arguments:
- queries: bfloat16 [2048, 4096], P('ctx', 'head'), may hold values from -5 to 5
- keys: bfloat16 [2048, 4096], P('ctx', 'head'), may hold values from -5 to 5
- values: bfloat16 [2048, 4096], P('ctx', 'head'), may hold values from -1300 to 1300
- gate_logits: bfloat16 [2048, 4096], P('ctx', 'head'), may hold values from -6 to 6
- norm_gain: float32 [4096], replicated, may hold values from 0.1 to 1.9
- out_weight: bfloat16 [4096, 6144], P(None, 'head'), may hold values from -0.09375 to 0.09375
- residual: bfloat16 [2048, 6144], P('ctx', 'head'), may hold values from -4 to 4
Outputs:
- layer_out: bfloat16 [2048, 6144], P('ctx', 'head')
The draws below stay inside these ranges and needn't reach their ends.
All inputs are finite; a program needn't handle non-finite values.
Results may differ from the reference program's by a relative error of at most 0.011.
Values may be sent and summed in bfloat16 or wider, within the bound.
A program may use at most 64 MiB of HBM per device.

```python
import math
import jax
import jax.numpy as jnp
from jax import lax

D = 6144
HEAD_DIM = 128
HEADS = 32
BLOCK = 256
INNER = 4096
SEQ = 2048


def draw_values(key, part):
    base_key = jax.random.fold_in(key, 7)
    entry_key, row_key, jitter_key = jax.random.split(base_key, 3)
    column_head = jnp.arange(INNER) // HEAD_DIM
    position = column_head.astype(jnp.float32) / max(HEADS - 1, 1)
    jitter = jnp.exp(jax.random.uniform(jitter_key, (HEADS,), jnp.float32, -0.2, 0.2))[column_head]
    row_scale = jnp.exp(jax.random.uniform(row_key, (SEQ, 1), jnp.float32, 0.0, math.log(10.0)))
    entries = jnp.clip(jax.random.normal(entry_key, (SEQ, INNER), jnp.float32), -4.0, 4.0)
    column_scale = 10.0 ** position
    return (entries * column_scale[None, :] * jitter[None, :] * row_scale).astype(jnp.bfloat16)


def block_scale(rng, extent, cuts, least, largest):
    gain, own = 1.0, jax.random.fold_in(rng, 6)
    for axis_at, parts in cuts:
        heights = jnp.exp(jax.random.uniform(jax.random.fold_in(own, axis_at), (parts,), jnp.float32, least / len(cuts), largest / len(cuts)))
        gain = gain * jnp.repeat(heights, extent[axis_at] // parts).reshape([-1 if axis == axis_at else 1 for axis in range(len(extent))])
    return gain


def scatter_about(stream_key, extent, scale, most, pieces=(), kind=jnp.bfloat16):
    values = scale * jax.random.normal(stream_key, extent, jnp.float32)
    if pieces:
        values = values * block_scale(stream_key, extent, pieces, -0.22, 0.18)
    return jnp.clip(values, -most, most).astype(kind)


def setup_inputs(seed: int = 0) -> dict:
    key_list = jax.random.split(jax.random.key(seed), 8)
    queries = scatter_about(key_list[0], (SEQ, INNER), 1.0, 5.0, ((0, 8), (1, 4)))
    keys = scatter_about(key_list[1], (SEQ, INNER), 1.0, 5.0, ((0, 8), (1, 4)))
    values = draw_values(jax.random.fold_in(key_list[7], 71), 0)
    gate_logits = scatter_about(key_list[3], (SEQ, INNER), 1.5, 6.0, ((0, 8), (1, 4)))
    norm_gain = jnp.clip(1.0 + 0.18 * jax.random.normal(key_list[4], (INNER,), jnp.float32), 0.1, 1.9)
    out_weight = scatter_about(key_list[5], (INNER, D), INNER ** -0.5, 0.09375, ((1, 4),))
    residual = scatter_about(key_list[6], (SEQ, D), 0.5, 4.0, ((0, 8), (1, 4)))
    return dict(queries=queries, keys=keys, values=values, gate_logits=gate_logits, norm_gain=norm_gain, out_weight=out_weight, residual=residual)


epsilon = 1e-06

def reference(queries, keys, values, gate_logits, norm_gain, out_weight, residual):
    block_count = SEQ // BLOCK
    query_blocks = queries.reshape(block_count, BLOCK, HEADS, HEAD_DIM)
    key_blocks = keys.reshape(block_count, BLOCK, HEADS, HEAD_DIM)
    value_blocks = values.reshape(block_count, BLOCK, HEADS, HEAD_DIM)
    causal_mask = jnp.tril(jnp.ones((BLOCK, BLOCK), dtype=bool))

    def advance(state_sum, block_inputs):
        query_part, key_part, value_part = block_inputs
        query_float = query_part.astype(jnp.float32)
        key_float = key_part.astype(jnp.float32)
        value_float = value_part.astype(jnp.float32)
        scores = jnp.einsum('thd,shd->hts', query_float, key_float, precision=lax.Precision.HIGHEST)
        scores = jnp.where(causal_mask[None], scores, jnp.float32(0.0)).astype(jnp.bfloat16)
        scores = lax.optimization_barrier(scores).astype(jnp.float32)
        local_part = jnp.einsum('hts,shd->thd', scores, value_float, precision=lax.Precision.HIGHEST)
        carried_part = jnp.einsum('thd,hde->the', query_float, state_sum, precision=lax.Precision.HIGHEST)
        block_state = jnp.einsum('shd,she->hde', key_float, value_float, precision=lax.Precision.HIGHEST)
        return (state_sum + block_state, (local_part + carried_part).astype(jnp.bfloat16))
    start_state = jnp.zeros((HEADS, HEAD_DIM, HEAD_DIM), jnp.float32)
    final_state, attended = lax.scan(advance, start_state, (query_blocks, key_blocks, value_blocks))
    attended = attended.reshape(SEQ, INNER).astype(jnp.float32)
    mean_square = lax.optimization_barrier(jnp.sum(attended * attended, axis=1)) / INNER
    scale_rows = lax.rsqrt(mean_square + epsilon)
    normed = attended * scale_rows[:, None] * norm_gain[None, :] * jax.nn.sigmoid(gate_logits.astype(jnp.float32))
    normed = normed.astype(jnp.bfloat16)
    projected = jnp.dot(normed, out_weight, preferred_element_type=jnp.float32)
    return (projected + residual.astype(jnp.float32)).astype(jnp.bfloat16)
```

```python
import functools

import jax
import jax.numpy as jnp
from jax import lax
from jax.experimental import pallas as pl
from jax.experimental.pallas import tpu as pltpu
from jax.sharding import PartitionSpec as P

HEAD_DIM = 128
EPSILON = 1e-06
MESH = pl.DeviceIdType.MESH
F32 = jnp.float32
BF16 = jnp.bfloat16


def kernel(
    steps, n_head, group,
    q_hbm, k_hbm, v_hbm, gate_hbm, gain_ref, w_hbm, res_hbm, out_ref,
    qb, kb, vb, gb, rb, wb, yall, acc, loc, tot, pre, st_send, st_recv, sq, ms,
    in_sem, w_sem, st_ssem, st_rsem, z_ssem, z_rsem, ms_ssem, ms_rsem,
):
    rows, width = qb.shape
    heads = width // HEAD_DIM
    groups = heads // group
    group_width = group * HEAD_DIM
    out_width = out_ref.shape[1]
    me_c = lax.axis_index("ctx")
    me_h = lax.axis_index("head")

    loads = [
        pltpu.make_async_copy(source, target, in_sem.at[number])
        for number, (source, target) in enumerate(
            ((k_hbm, kb), (v_hbm, vb), (q_hbm, qb), (gate_hbm, gb), (res_hbm, rb))
        )
    ]
    w_loads = [
        pltpu.make_async_copy(
            w_hbm.at[pl.ds(o * width, width)], wb.at[pl.ds(o * width, width)], w_sem.at[o]
        )
        for o in range(n_head)
    ]
    for load in loads:
        load.start()

    def bit(step):
        return lax.rem(me_c // (2**step), 2)

    def partner(step):
        return me_c + (2**step) * (1 - 2 * bit(step))

    barrier = pltpu.get_barrier_semaphore()
    for step in range(steps):
        pl.semaphore_signal(
            barrier, inc=1, device_id={"ctx": partner(step)}, device_id_type=MESH
        )
    for d in range(1, n_head):
        pl.semaphore_signal(
            barrier, inc=1, device_id={"head": lax.rem(me_h + d, n_head)}, device_id_type=MESH
        )

    def state_rows(g):
        return pl.ds(g * group_width, group_width)

    def state_copy(step, g):
        return pltpu.make_async_remote_copy(
            src_ref=st_send.at[step, state_rows(g)],
            dst_ref=st_recv.at[step, state_rows(g)],
            send_sem=st_ssem.at[step, g],
            recv_sem=st_rsem.at[step, g],
            device_id={"ctx": partner(step)},
            device_id_type=MESH,
        )

    def send_state(step, g):
        st_send[step, state_rows(g), :] = tot[state_rows(g), :].astype(BF16)
        state_copy(step, g).start()

    def head_cols(h):
        return pl.ds(h * HEAD_DIM, HEAD_DIM)

    loads[0].wait()
    loads[1].wait()
    for load in w_loads:
        load.start()

    def own_state(g):
        for h in range(g * group, (g + 1) * group):
            tot[head_cols(h), :] = lax.dot_general(
                kb[:, head_cols(h)], vb[:, head_cols(h)], (((0,), (0,)), ((), ())),
                preferred_element_type=F32,
            )

    own_state(0)
    pl.semaphore_wait(barrier, steps + n_head - 1)
    for g in range(groups):
        if g > 0:
            own_state(g)
        send_state(0, g)
    pre[...] = jnp.zeros_like(pre)
    sq[...] = jnp.zeros_like(sq)
    loads[2].wait()
    loads[3].wait()

    def local(g):
        at = lax.broadcasted_iota(jnp.int32, (rows, rows), 0)
        of = lax.broadcasted_iota(jnp.int32, (rows, rows), 1)
        for h in range(g * group, (g + 1) * group):
            scores = lax.dot_general(
                qb[:, head_cols(h)], kb[:, head_cols(h)], (((1,), (1,)), ((), ())),
                preferred_element_type=F32,
            )
            scores = jnp.where(of <= at, scores, 0.0).astype(BF16)
            loc[:, head_cols(h)] = jnp.dot(
                scores, vb[:, head_cols(h)], preferred_element_type=F32
            )

    def z_copy(way, hop, c, origin):
        return pltpu.make_async_remote_copy(
            src_ref=yall.at[origin, c],
            dst_ref=yall.at[origin, c],
            send_sem=z_ssem.at[way, hop - 1, c],
            recv_sem=z_rsem.at[way, hop - 1, c],
            device_id={"head": me_h + 1 - 2 * way},
            device_id_type=MESH,
        )

    def finish(g):
        for number in range(group):
            h = g * group + number
            carried = jnp.dot(
                qb[:, head_cols(h)], pre[head_cols(h), :].astype(BF16),
                preferred_element_type=F32,
            )
            attended = (loc[:, head_cols(h)] + carried).astype(BF16).astype(F32)
            sq[...] += attended * attended
            gain = gain_ref[:, pl.ds(pl.multiple_of(me_h * width + h * HEAD_DIM, HEAD_DIM), HEAD_DIM)]
            gate = gb[:, head_cols(h)].astype(F32)
            yall[me_h, g, :, head_cols(number)] = (
                attended * gain * (1.0 / (1.0 + jnp.exp(-gate)))
            ).astype(BF16)

        @pl.when(me_h < n_head - 1)
        def _():
            z_copy(0, 1, g, me_h).start()

        @pl.when(me_h > 0)
        def _():
            z_copy(1, 1, g, me_h).start()

    for wave in range(max(groups, groups + steps - 1)):
        if wave < groups:
            local(wave)
        for step in reversed(range(steps)):
            g = wave - step
            if not 0 <= g < groups:
                continue
            state_copy(step, g).wait_recv()
            got = st_recv[step, state_rows(g), :].astype(F32)
            if step < steps - 1:
                tot[state_rows(g), :] += got
                send_state(step + 1, g)
            pre[state_rows(g), :] += jnp.where(bit(step) == 1, got, 0.0)
            if step == steps - 1:
                finish(g)
        if steps == 0:
            finish(wave)

    def ms_copy(d, source):
        return pltpu.make_async_remote_copy(
            src_ref=ms.at[source],
            dst_ref=ms.at[source],
            send_sem=ms_ssem.at[d],
            recv_sem=ms_rsem.at[d],
            device_id={"head": lax.rem(me_h + d, n_head)},
            device_id_type=MESH,
        )

    row_total = jnp.sum(jnp.transpose(sq[...]), axis=0, keepdims=True)
    ms[me_h] = jnp.broadcast_to(row_total, ms.shape[1:])
    for d in range(1, n_head):
        ms_copy(d, me_h).start()
    acc[...] = jnp.zeros_like(acc)
    loads[4].wait()
    for load in w_loads:
        load.wait()

    def project(origin, c):
        at = pl.multiple_of(origin * width + c * group_width, group_width)
        acc[...] += jnp.dot(
            yall[origin, c], wb[pl.ds(at, group_width), :], preferred_element_type=F32
        )

    for d in range(1, n_head):
        def arrive(c, carry, d=d):
            @pl.when(me_h - d >= 0)
            def _():
                z_copy(0, d, c, me_h - d).wait_recv()

                @pl.when(me_h < n_head - 1)
                def _():
                    z_copy(0, d + 1, c, me_h - d).start()

            @pl.when(me_h + d < n_head)
            def _():
                z_copy(1, d, c, me_h + d).wait_recv()

                @pl.when(me_h > 0)
                def _():
                    z_copy(1, d + 1, c, me_h + d).start()

            if d == 1:
                project(me_h, c)

            @pl.when(me_h - d >= 0)
            def _():
                project(me_h - d, c)

            @pl.when(me_h + d < n_head)
            def _():
                project(me_h + d, c)

            return carry

        lax.fori_loop(0, groups, arrive, 0)

    for d in range(1, n_head):
        ms_copy(d, lax.rem(me_h + n_head - d, n_head)).wait_recv()
    total = ms[0, 0:1, :]
    for o in range(1, n_head):
        total = total + ms[o, 0:1, :]
    scale = lax.rsqrt(total / (n_head * width) + EPSILON)
    scale = jnp.transpose(jnp.broadcast_to(scale, (HEAD_DIM, rows)))
    for j in range(out_width // HEAD_DIM):
        out_ref[:, head_cols(j)] = (
            acc[:, head_cols(j)] * scale + rb[:, head_cols(j)].astype(F32)
        ).astype(out_ref.dtype)

    for step in range(steps):
        for g in range(groups):
            state_copy(step, g).wait_send()
    for d in range(1, n_head):
        ms_copy(d, me_h).wait_send()
        for c in range(groups):
            @pl.when(jnp.logical_and(me_h < n_head - 1, me_h - (d - 1) >= 0))
            def _(c=c, d=d):
                z_copy(0, d, c, me_h - (d - 1)).wait_send()

            @pl.when(jnp.logical_and(me_h > 0, me_h + (d - 1) < n_head))
            def _(c=c, d=d):
                z_copy(1, d, c, me_h + (d - 1)).wait_send()


def solution(mesh):
    n_ctx, n_head = mesh.shape["ctx"], mesh.shape["head"]
    steps = n_ctx.bit_length() - 1
    assert n_ctx == 2**steps

    def on_device(queries, keys, values, gate_logits, norm_gain, out_weight, residual):
        rows, width = queries.shape
        inner, out_width = out_weight.shape
        heads = width // HEAD_DIM
        group = 2 if heads % 2 == 0 else 1
        groups = heads // group
        group_width = group * HEAD_DIM
        anywhere = pl.BlockSpec(memory_space=pl.ANY)
        vmem = pl.BlockSpec(memory_space=pltpu.VMEM)
        dma = pltpu.SemaphoreType.DMA
        hops = max(n_head - 1, 1)
        stages = max(steps, 1)
        return pl.pallas_call(
            functools.partial(kernel, steps, n_head, group),
            out_shape=jax.ShapeDtypeStruct((rows, out_width), residual.dtype),
            in_specs=[anywhere] * 4 + [vmem] + [anywhere] * 2,
            out_specs=vmem,
            scratch_shapes=[
                pltpu.VMEM((rows, width), BF16),
                pltpu.VMEM((rows, width), BF16),
                pltpu.VMEM((rows, width), BF16),
                pltpu.VMEM((rows, width), BF16),
                pltpu.VMEM((rows, out_width), BF16),
                pltpu.VMEM((inner, out_width), BF16),
                pltpu.VMEM((n_head, groups, rows, group_width), BF16),
                pltpu.VMEM((rows, out_width), F32),
                pltpu.VMEM((rows, width), F32),
                pltpu.VMEM((width, HEAD_DIM), F32),
                pltpu.VMEM((width, HEAD_DIM), F32),
                pltpu.VMEM((stages, width, HEAD_DIM), BF16),
                pltpu.VMEM((stages, width, HEAD_DIM), BF16),
                pltpu.VMEM((rows, HEAD_DIM), F32),
                pltpu.VMEM((n_head, 8, rows), F32),
                dma((5,)),
                dma((n_head,)),
                dma((stages, groups)),
                dma((stages, groups)),
                dma((2, hops, groups)),
                dma((2, hops, groups)),
                dma((n_head,)),
                dma((n_head,)),
            ],
            compiler_params=pltpu.CompilerParams(
                collective_id=0, has_side_effects=True, vmem_limit_bytes=48 * 1024 * 1024
            ),
        )(queries, keys, values, gate_logits, norm_gain[None, :], out_weight, residual)

    in_specs = (
        P("ctx", "head"),
        P("ctx", "head"),
        P("ctx", "head"),
        P("ctx", "head"),
        P(),
        P(None, "head"),
        P("ctx", "head"),
    )
    return jax.shard_map(
        on_device, mesh=mesh, in_specs=in_specs, out_specs=P("ctx", "head"), check_vma=False
    )
```

```python
import functools

import jax
import jax.numpy as jnp
from jax import lax
from jax.experimental import pallas as pl
from jax.experimental.pallas import tpu as pltpu
from jax.sharding import PartitionSpec as P

HEAD_DIM = 128
EPSILON = 1e-06
MESH = pl.DeviceIdType.MESH
F32 = jnp.float32
BF16 = jnp.bfloat16


def kernel(
    steps, n_head, group,
    q_hbm, k_hbm, v_hbm, gate_hbm, gain_ref, w_hbm, res_hbm, out_ref,
    qb, kb, vb, gb, rb, wb, yall, acc, loc, tot, pre, st_send, st_recv, sq, ms,
    in_sem, w_sem, st_ssem, st_rsem, z_ssem, z_rsem, ms_ssem, ms_rsem,
):
    rows, width = qb.shape
    heads = width // HEAD_DIM
    groups = heads // group
    group_width = group * HEAD_DIM
    out_width = out_ref.shape[1]
    me_c = lax.axis_index("ctx")
    me_h = lax.axis_index("head")

    loads = [
        pltpu.make_async_copy(source, target, in_sem.at[number])
        for number, (source, target) in enumerate(
            ((k_hbm, kb), (v_hbm, vb), (q_hbm, qb), (gate_hbm, gb), (res_hbm, rb))
        )
    ]
    w_loads = [
        pltpu.make_async_copy(
            w_hbm.at[pl.ds(o * width, width)], wb.at[pl.ds(o * width, width)], w_sem.at[o]
        )
        for o in range(n_head)
    ]
    for load in loads:
        load.start()

    def bit(step):
        return lax.rem(me_c // (2**step), 2)

    def partner(step):
        return me_c + (2**step) * (1 - 2 * bit(step))

    barrier = pltpu.get_barrier_semaphore()
    for step in range(steps):
        pl.semaphore_signal(
            barrier, inc=1, device_id={"ctx": partner(step)}, device_id_type=MESH
        )
    for d in range(1, n_head):
        pl.semaphore_signal(
            barrier, inc=1, device_id={"head": lax.rem(me_h + d, n_head)}, device_id_type=MESH
        )

    def state_rows(g):
        return pl.ds(g * group_width, group_width)

    def state_copy(step, g):
        return pltpu.make_async_remote_copy(
            src_ref=st_send.at[step, state_rows(g)],
            dst_ref=st_recv.at[step, state_rows(g)],
            send_sem=st_ssem.at[step, g],
            recv_sem=st_rsem.at[step, g],
            device_id={"ctx": partner(step)},
            device_id_type=MESH,
        )

    def send_state(step, g):
        st_send[step, state_rows(g), :] = tot[state_rows(g), :].astype(BF16)
        state_copy(step, g).start()

    def head_cols(h):
        return pl.ds(h * HEAD_DIM, HEAD_DIM)

    loads[0].wait()
    loads[1].wait()
    for load in w_loads:
        load.start()

    def own_state(g):
        for h in range(g * group, (g + 1) * group):
            tot[head_cols(h), :] = lax.dot_general(
                kb[:, head_cols(h)], vb[:, head_cols(h)], (((0,), (0,)), ((), ())),
                preferred_element_type=F32,
            )

    own_state(0)
    pl.semaphore_wait(barrier, steps + n_head - 1)
    for g in range(groups):
        if g > 0:
            own_state(g)
        send_state(0, g)
    pre[...] = jnp.zeros_like(pre)
    sq[...] = jnp.zeros_like(sq)
    loads[2].wait()
    loads[3].wait()

    def local(g):
        at = lax.broadcasted_iota(jnp.int32, (rows, rows), 0)
        of = lax.broadcasted_iota(jnp.int32, (rows, rows), 1)
        for h in range(g * group, (g + 1) * group):
            scores = lax.dot_general(
                qb[:, head_cols(h)], kb[:, head_cols(h)], (((1,), (1,)), ((), ())),
                preferred_element_type=F32,
            )
            scores = jnp.where(of <= at, scores, 0.0).astype(BF16)
            loc[:, head_cols(h)] = jnp.dot(
                scores, vb[:, head_cols(h)], preferred_element_type=F32
            )

    def z_copy(way, hop, c, origin):
        return pltpu.make_async_remote_copy(
            src_ref=yall.at[origin, c],
            dst_ref=yall.at[origin, c],
            send_sem=z_ssem.at[way, hop - 1, c],
            recv_sem=z_rsem.at[way, hop - 1, c],
            device_id={"head": me_h + 1 - 2 * way},
            device_id_type=MESH,
        )

    def finish(g):
        for number in range(group):
            h = g * group + number
            carried = jnp.dot(
                qb[:, head_cols(h)], pre[head_cols(h), :].astype(BF16),
                preferred_element_type=F32,
            )
            attended = (loc[:, head_cols(h)] + carried).astype(BF16).astype(F32)
            sq[...] += attended * attended
            gain = gain_ref[:, pl.ds(pl.multiple_of(me_h * width + h * HEAD_DIM, HEAD_DIM), HEAD_DIM)]
            gate = gb[:, head_cols(h)].astype(F32)
            yall[me_h, g, :, head_cols(number)] = (
                attended * gain * (1.0 / (1.0 + jnp.exp(-gate)))
            ).astype(BF16)

        @pl.when(me_h < n_head - 1)
        def _():
            z_copy(0, 1, g, me_h).start()

        @pl.when(me_h > 0)
        def _():
            z_copy(1, 1, g, me_h).start()

    for wave in range(max(groups, groups + steps - 1)):
        if wave < groups:
            local(wave)
        for step in reversed(range(steps)):
            g = wave - step
            if not 0 <= g < groups:
                continue
            state_copy(step, g).wait_recv()
            got = st_recv[step, state_rows(g), :].astype(F32)
            if step < steps - 1:
                tot[state_rows(g), :] += got
                send_state(step + 1, g)
            pre[state_rows(g), :] += jnp.where(bit(step) == 1, got, 0.0)
            if step == steps - 1:
                finish(g)
        if steps == 0:
            finish(wave)

    def ms_copy(d, source):
        return pltpu.make_async_remote_copy(
            src_ref=ms.at[source],
            dst_ref=ms.at[source],
            send_sem=ms_ssem.at[d],
            recv_sem=ms_rsem.at[d],
            device_id={"head": lax.rem(me_h + d, n_head)},
            device_id_type=MESH,
        )

    row_total = jnp.sum(jnp.transpose(sq[...]), axis=0, keepdims=True)
    ms[me_h] = jnp.broadcast_to(row_total, ms.shape[1:])
    for d in range(1, n_head):
        ms_copy(d, me_h).start()
    acc[...] = jnp.zeros_like(acc)
    loads[4].wait()
    for load in w_loads:
        load.wait()

    def project(origin, c):
        at = pl.multiple_of(origin * width + c * group_width, group_width)
        acc[...] += jnp.dot(
            yall[origin, c], wb[pl.ds(at, group_width), :], preferred_element_type=F32
        )

    for d in range(1, n_head):
        def arrive(c, carry, d=d):
            @pl.when(me_h - d >= 0)
            def _():
                z_copy(0, d, c, me_h - d).wait_recv()

                @pl.when(me_h < n_head - 1)
                def _():
                    z_copy(0, d + 1, c, me_h - d).start()

            @pl.when(me_h + d < n_head)
            def _():
                z_copy(1, d, c, me_h + d).wait_recv()

                @pl.when(me_h > 0)
                def _():
                    z_copy(1, d + 1, c, me_h + d).start()

            if d == 1:
                project(me_h, c)

            @pl.when(me_h - d >= 0)
            def _():
                project(me_h - d, c)

            @pl.when(me_h + d < n_head)
            def _():
                project(me_h + d, c)

            return carry

        lax.fori_loop(0, groups, arrive, 0)

    for d in range(1, n_head):
        ms_copy(d, lax.rem(me_h + n_head - d, n_head)).wait_recv()
    total = ms[0, 0:1, :]
    for o in range(1, n_head):
        total = total + ms[o, 0:1, :]
    scale = lax.rsqrt(total / (n_head * width) + EPSILON)
    scale = jnp.transpose(jnp.broadcast_to(scale, (HEAD_DIM, rows)))
    for j in range(out_width // HEAD_DIM):
        out_ref[:, head_cols(j)] = (
            acc[:, head_cols(j)] * scale + rb[:, head_cols(j)].astype(F32)
        ).astype(out_ref.dtype)

    for step in range(steps):
        for g in range(groups):
            state_copy(step, g).wait_send()
    for d in range(1, n_head):
        ms_copy(d, me_h).wait_send()
        for c in range(groups):
            @pl.when(jnp.logical_and(me_h < n_head - 1, me_h - (d - 1) >= 0))
            def _(c=c, d=d):
                z_copy(0, d, c, me_h - (d - 1)).wait_send()

            @pl.when(jnp.logical_and(me_h > 0, me_h + (d - 1) < n_head))
            def _(c=c, d=d):
                z_copy(1, d, c, me_h + (d - 1)).wait_send()


def solution(mesh):
    n_ctx, n_head = mesh.shape["ctx"], mesh.shape["head"]
    steps = n_ctx.bit_length() - 1
    assert n_ctx == 2**steps

    def on_device(queries, keys, values, gate_logits, norm_gain, out_weight, residual):
        rows, width = queries.shape
        inner, out_width = out_weight.shape
        heads = width // HEAD_DIM
        group = 2 if heads % 2 == 0 else 1
        groups = heads // group
        group_width = group * HEAD_DIM
        anywhere = pl.BlockSpec(memory_space=pl.ANY)
        vmem = pl.BlockSpec(memory_space=pltpu.VMEM)
        dma = pltpu.SemaphoreType.DMA
        hops = max(n_head - 1, 1)
        stages = max(steps, 1)
        return pl.pallas_call(
            functools.partial(kernel, steps, n_head, group),
            out_shape=jax.ShapeDtypeStruct((rows, out_width), residual.dtype),
            in_specs=[anywhere] * 4 + [vmem] + [anywhere] * 2,
            out_specs=vmem,
            scratch_shapes=[
                pltpu.VMEM((rows, width), BF16),
                pltpu.VMEM((rows, width), BF16),
                pltpu.VMEM((rows, width), BF16),
                pltpu.VMEM((rows, width), BF16),
                pltpu.VMEM((rows, out_width), BF16),
                pltpu.VMEM((inner, out_width), BF16),
                pltpu.VMEM((n_head, groups, rows, group_width), BF16),
                pltpu.VMEM((rows, out_width), F32),
                pltpu.VMEM((rows, width), F32),
                pltpu.VMEM((width, HEAD_DIM), F32),
                pltpu.VMEM((width, HEAD_DIM), F32),
                pltpu.VMEM((stages, width, HEAD_DIM), BF16),
                pltpu.VMEM((stages, width, HEAD_DIM), BF16),
                pltpu.VMEM((rows, HEAD_DIM), F32),
                pltpu.VMEM((n_head, 8, rows), F32),
                dma((5,)),
                dma((n_head,)),
                dma((stages, groups)),
                dma((stages, groups)),
                dma((2, hops, groups)),
                dma((2, hops, groups)),
                dma((n_head,)),
                dma((n_head,)),
            ],
            compiler_params=pltpu.CompilerParams(
                collective_id=0, has_side_effects=True, vmem_limit_bytes=62 * 1024 * 1024
            ),
        )(queries, keys, values, gate_logits, norm_gain[None, :], out_weight, residual)

    in_specs = (
        P("ctx", "head"),
        P("ctx", "head"),
        P("ctx", "head"),
        P("ctx", "head"),
        P(),
        P(None, "head"),
        P("ctx", "head"),
    )
    return jax.shard_map(
        on_device, mesh=mesh, in_specs=in_specs, out_specs=P("ctx", "head"), check_vma=False
    )
```

```python
import functools

import jax
import jax.numpy as jnp
from jax import lax
from jax.experimental import pallas as pl
from jax.experimental.pallas import tpu as pltpu
from jax.sharding import PartitionSpec as P

HEAD_DIM = 128
EPSILON = 1e-06
MESH = pl.DeviceIdType.MESH
F32 = jnp.float32
BF16 = jnp.bfloat16


def kernel(
    stages, n_head, group,
    q_hbm, k_hbm, v_hbm, gate_hbm, gain_ref, w_hbm, res_hbm, out_ref,
    qb, kb, vb, gb, rb, wb, yall, acc, loc, tot, pre, st_send, st_recv, sq, ms,
    in_sem, w_sem, st_ssem, st_rsem, z_ssem, z_rsem, ms_ssem, ms_rsem,
):
    rows, width = qb.shape
    heads = width // HEAD_DIM
    groups = heads // group
    group_width = group * HEAD_DIM
    out_width = out_ref.shape[1]
    me_c = lax.axis_index("ctx")
    me_h = lax.axis_index("head")

    loads = [
        pltpu.make_async_copy(source, target, in_sem.at[number])
        for number, (source, target) in enumerate(
            ((k_hbm, kb), (v_hbm, vb), (q_hbm, qb), (gate_hbm, gb), (res_hbm, rb))
        )
    ]
    w_loads = [
        pltpu.make_async_copy(
            w_hbm.at[pl.ds(o * width, width)], wb.at[pl.ds(o * width, width)], w_sem.at[o]
        )
        for o in range(n_head)
    ]
    for load in loads:
        load.start()

    slots, last = [], len(stages) - 1
    for stage, (weight, radix) in enumerate(stages):
        slots.append([])
        for m in range(1, radix):
            slots[stage].append((sum(map(len, slots)), m))

    def digit(stage):
        weight, radix = stages[stage]
        return lax.rem(me_c // weight, radix)

    def partner(stage, m):
        weight, radix = stages[stage]
        own = digit(stage)
        return me_c + weight * (lax.rem(own + m, radix) - own)

    barrier = pltpu.get_barrier_semaphore()
    for stage in range(len(stages)):
        for _, m in slots[stage]:
            pl.semaphore_signal(
                barrier, inc=1, device_id={"ctx": partner(stage, m)}, device_id_type=MESH
            )
    for d in range(1, n_head):
        pl.semaphore_signal(
            barrier, inc=1, device_id={"head": lax.rem(me_h + d, n_head)}, device_id_type=MESH
        )

    def state_rows(g):
        return pl.ds(g * group_width, group_width)

    def state_copy(stage, slot, m, g):
        return pltpu.make_async_remote_copy(
            src_ref=st_send.at[stage, state_rows(g)],
            dst_ref=st_recv.at[slot, state_rows(g)],
            send_sem=st_ssem.at[slot, g],
            recv_sem=st_rsem.at[slot, g],
            device_id={"ctx": partner(stage, m)},
            device_id_type=MESH,
        )

    def to_later(stage, m, act):
        if stage < last:
            act()
        else:
            pl.when(digit(stage) + m < stages[stage][1])(act)

    def from_earlier(stage, m, act):
        if stage < last:
            act()
        else:
            pl.when(digit(stage) - m >= 0)(act)

    def send_state(stage, g):
        st_send[stage, state_rows(g), :] = tot[state_rows(g), :].astype(BF16)
        for slot, m in slots[stage]:
            to_later(stage, m, lambda: state_copy(stage, slot, m, g).start())

    def take_state(stage, g):
        for slot, m in slots[stage]:
            def take():
                state_copy(stage, slot, m, g).wait_recv()
                got = st_recv[slot, state_rows(g), :].astype(F32)
                if stage < last:
                    tot[state_rows(g), :] += got
                    got = jnp.where(digit(stage) >= m, got, 0.0)
                pre[state_rows(g), :] += got

            from_earlier(stage, m, take)

    def head_cols(h):
        return pl.ds(h * HEAD_DIM, HEAD_DIM)

    loads[0].wait()
    loads[1].wait()
    for load in w_loads:
        load.start()

    def own_state(g):
        for h in range(g * group, (g + 1) * group):
            tot[head_cols(h), :] = lax.dot_general(
                kb[:, head_cols(h)], vb[:, head_cols(h)], (((0,), (0,)), ((), ())),
                preferred_element_type=F32,
            )

    own_state(0)
    pl.semaphore_wait(barrier, sum(map(len, slots)) + n_head - 1)
    for g in range(groups):
        if g > 0:
            own_state(g)
        if stages:
            send_state(0, g)
    pre[...] = jnp.zeros_like(pre)
    sq[...] = jnp.zeros_like(sq)
    loads[2].wait()
    loads[3].wait()

    def local(g):
        at = lax.broadcasted_iota(jnp.int32, (rows, rows), 0)
        of = lax.broadcasted_iota(jnp.int32, (rows, rows), 1)
        for h in range(g * group, (g + 1) * group):
            scores = lax.dot_general(
                qb[:, head_cols(h)], kb[:, head_cols(h)], (((1,), (1,)), ((), ())),
                preferred_element_type=F32,
            )
            scores = jnp.where(of <= at, scores, 0.0).astype(BF16)
            loc[:, head_cols(h)] = jnp.dot(
                scores, vb[:, head_cols(h)], preferred_element_type=F32
            )

    def z_copy(way, hop, c, origin):
        return pltpu.make_async_remote_copy(
            src_ref=yall.at[origin, c],
            dst_ref=yall.at[origin, c],
            send_sem=z_ssem.at[way, hop - 1, c],
            recv_sem=z_rsem.at[way, hop - 1, c],
            device_id={"head": me_h + 1 - 2 * way},
            device_id_type=MESH,
        )

    def finish(g):
        for number in range(group):
            h = g * group + number
            carried = jnp.dot(
                qb[:, head_cols(h)], pre[head_cols(h), :].astype(BF16),
                preferred_element_type=F32,
            )
            attended = (loc[:, head_cols(h)] + carried).astype(BF16).astype(F32)
            sq[...] += attended * attended
            gain = gain_ref[:, pl.ds(pl.multiple_of(me_h * width + h * HEAD_DIM, HEAD_DIM), HEAD_DIM)]
            gate = gb[:, head_cols(h)].astype(F32)
            yall[me_h, g, :, head_cols(number)] = (
                attended * gain * (1.0 / (1.0 + jnp.exp(-gate)))
            ).astype(BF16)

        @pl.when(me_h < n_head - 1)
        def _():
            z_copy(0, 1, g, me_h).start()

        @pl.when(me_h > 0)
        def _():
            z_copy(1, 1, g, me_h).start()

    for stage in range(last):
        for g in range(groups):
            take_state(stage, g)
            send_state(stage + 1, g)
    for g in range(groups):
        local(g)
    for g in range(groups):
        if stages:
            take_state(last, g)
        finish(g)

    def ms_copy(d, source):
        return pltpu.make_async_remote_copy(
            src_ref=ms.at[source],
            dst_ref=ms.at[source],
            send_sem=ms_ssem.at[d],
            recv_sem=ms_rsem.at[d],
            device_id={"head": lax.rem(me_h + d, n_head)},
            device_id_type=MESH,
        )

    row_total = jnp.sum(jnp.transpose(sq[...]), axis=0, keepdims=True)
    ms[me_h] = jnp.broadcast_to(row_total, ms.shape[1:])
    for d in range(1, n_head):
        ms_copy(d, me_h).start()
    acc[...] = jnp.zeros_like(acc)
    loads[4].wait()
    for load in w_loads:
        load.wait()

    def project(origin, c):
        at = pl.multiple_of(origin * width + c * group_width, group_width)
        acc[...] += jnp.dot(
            yall[origin, c], wb[pl.ds(at, group_width), :], preferred_element_type=F32
        )

    for d in range(1, n_head):
        def arrive(c, carry, d=d):
            @pl.when(me_h - d >= 0)
            def _():
                z_copy(0, d, c, me_h - d).wait_recv()

                @pl.when(me_h < n_head - 1)
                def _():
                    z_copy(0, d + 1, c, me_h - d).start()

            @pl.when(me_h + d < n_head)
            def _():
                z_copy(1, d, c, me_h + d).wait_recv()

                @pl.when(me_h > 0)
                def _():
                    z_copy(1, d + 1, c, me_h + d).start()

            if d == 1:
                project(me_h, c)

            @pl.when(me_h - d >= 0)
            def _():
                project(me_h - d, c)

            @pl.when(me_h + d < n_head)
            def _():
                project(me_h + d, c)

            return carry

        lax.fori_loop(0, groups, arrive, 0)

    for d in range(1, n_head):
        ms_copy(d, lax.rem(me_h + n_head - d, n_head)).wait_recv()
    total = ms[0, 0:1, :]
    for o in range(1, n_head):
        total = total + ms[o, 0:1, :]
    scale = lax.rsqrt(total / (n_head * width) + EPSILON)
    scale = jnp.transpose(jnp.broadcast_to(scale, (HEAD_DIM, rows)))
    for j in range(out_width // HEAD_DIM):
        out_ref[:, head_cols(j)] = (
            acc[:, head_cols(j)] * scale + rb[:, head_cols(j)].astype(F32)
        ).astype(out_ref.dtype)

    for stage in range(len(stages)):
        for slot, m in slots[stage]:
            for g in range(groups):
                to_later(stage, m, lambda: state_copy(stage, slot, m, g).wait_send())
    for d in range(1, n_head):
        ms_copy(d, me_h).wait_send()
        for c in range(groups):
            @pl.when(jnp.logical_and(me_h < n_head - 1, me_h - (d - 1) >= 0))
            def _(c=c, d=d):
                z_copy(0, d, c, me_h - (d - 1)).wait_send()

            @pl.when(jnp.logical_and(me_h > 0, me_h + (d - 1) < n_head))
            def _(c=c, d=d):
                z_copy(1, d, c, me_h + (d - 1)).wait_send()


def solution(mesh):
    n_ctx, n_head = mesh.shape["ctx"], mesh.shape["head"]
    steps = n_ctx.bit_length() - 1
    assert n_ctx == 2**steps
    stages = [(1, 2)] if steps % 2 else []
    for bit in range(steps % 2, steps, 2):
        stages.append((2**bit, 4))

    def on_device(queries, keys, values, gate_logits, norm_gain, out_weight, residual):
        rows, width = queries.shape
        inner, out_width = out_weight.shape
        heads = width // HEAD_DIM
        group = 2 if heads % 2 == 0 else 1
        groups = heads // group
        group_width = group * HEAD_DIM
        anywhere = pl.BlockSpec(memory_space=pl.ANY)
        vmem = pl.BlockSpec(memory_space=pltpu.VMEM)
        dma = pltpu.SemaphoreType.DMA
        hops = max(n_head - 1, 1)
        stage_count = max(len(stages), 1)
        slot_count = max(sum(radix - 1 for _, radix in stages), 1)
        return pl.pallas_call(
            functools.partial(kernel, tuple(stages), n_head, group),
            out_shape=jax.ShapeDtypeStruct((rows, out_width), residual.dtype),
            in_specs=[anywhere] * 4 + [vmem] + [anywhere] * 2,
            out_specs=vmem,
            scratch_shapes=[
                pltpu.VMEM((rows, width), BF16),
                pltpu.VMEM((rows, width), BF16),
                pltpu.VMEM((rows, width), BF16),
                pltpu.VMEM((rows, width), BF16),
                pltpu.VMEM((rows, out_width), BF16),
                pltpu.VMEM((inner, out_width), BF16),
                pltpu.VMEM((n_head, groups, rows, group_width), BF16),
                pltpu.VMEM((rows, out_width), F32),
                pltpu.VMEM((rows, width), F32),
                pltpu.VMEM((width, HEAD_DIM), F32),
                pltpu.VMEM((width, HEAD_DIM), F32),
                pltpu.VMEM((stage_count, width, HEAD_DIM), BF16),
                pltpu.VMEM((slot_count, width, HEAD_DIM), BF16),
                pltpu.VMEM((rows, HEAD_DIM), F32),
                pltpu.VMEM((n_head, 8, rows), F32),
                dma((5,)),
                dma((n_head,)),
                dma((slot_count, groups)),
                dma((slot_count, groups)),
                dma((2, hops, groups)),
                dma((2, hops, groups)),
                dma((n_head,)),
                dma((n_head,)),
            ],
            compiler_params=pltpu.CompilerParams(
                collective_id=0, has_side_effects=True, vmem_limit_bytes=62 * 1024 * 1024
            ),
        )(queries, keys, values, gate_logits, norm_gain[None, :], out_weight, residual)

    in_specs = (
        P("ctx", "head"),
        P("ctx", "head"),
        P("ctx", "head"),
        P("ctx", "head"),
        P(),
        P(None, "head"),
        P("ctx", "head"),
    )
    return jax.shard_map(
        on_device, mesh=mesh, in_specs=in_specs, out_specs=P("ctx", "head"), check_vma=False
    )
```

```python
import functools

import jax
import jax.numpy as jnp
from jax import lax
from jax.experimental import pallas as pl
from jax.experimental.pallas import tpu as pltpu
from jax.sharding import PartitionSpec as P

HEAD_DIM = 128
EPSILON = 1e-06
MESH = pl.DeviceIdType.MESH
F32 = jnp.float32
BF16 = jnp.bfloat16


def kernel(
    stages, n_head, group,
    q_hbm, k_hbm, v_hbm, gate_hbm, gain_ref, w_hbm, res_hbm, out_ref,
    qb, kb, vb, gb, rb, wb, yall, acc, loc, tot, pre, st_send, st_recv, sq, ms,
    in_sem, w_sem, st_ssem, st_rsem, z_ssem, z_rsem, ms_ssem, ms_rsem,
):
    rows, width = qb.shape
    heads = width // HEAD_DIM
    groups = heads // group
    group_width = group * HEAD_DIM
    out_width = out_ref.shape[1]
    me_c = lax.axis_index("ctx")
    me_h = lax.axis_index("head")

    loads = [
        pltpu.make_async_copy(source, target, in_sem.at[number])
        for number, (source, target) in enumerate(
            ((k_hbm, kb), (v_hbm, vb), (q_hbm, qb), (gate_hbm, gb), (res_hbm, rb))
        )
    ]
    w_loads = [
        pltpu.make_async_copy(
            w_hbm.at[pl.ds(o * width, width)], wb.at[pl.ds(o * width, width)], w_sem.at[o]
        )
        for o in range(n_head)
    ]
    for load in loads:
        load.start()

    slots, last = [], len(stages) - 1
    for stage, (weight, radix) in enumerate(stages):
        slots.append([])
        for m in range(1, radix):
            slots[stage].append((sum(map(len, slots)), m))

    def digit(stage):
        weight, radix = stages[stage]
        return lax.rem(me_c // weight, radix)

    def partner(stage, m):
        weight, radix = stages[stage]
        own = digit(stage)
        return me_c + weight * (lax.rem(own + m, radix) - own)

    barrier = pltpu.get_barrier_semaphore()
    for stage in range(len(stages)):
        for _, m in slots[stage]:
            pl.semaphore_signal(
                barrier, inc=1, device_id={"ctx": partner(stage, m)}, device_id_type=MESH
            )
    for d in range(1, n_head):
        pl.semaphore_signal(
            barrier, inc=1, device_id={"head": lax.rem(me_h + d, n_head)}, device_id_type=MESH
        )

    def state_rows(g):
        return pl.ds(g * group_width, group_width)

    def state_copy(stage, slot, m, g):
        return pltpu.make_async_remote_copy(
            src_ref=st_send.at[stage, state_rows(g)],
            dst_ref=st_recv.at[slot, state_rows(g)],
            send_sem=st_ssem.at[slot, g],
            recv_sem=st_rsem.at[slot, g],
            device_id={"ctx": partner(stage, m)},
            device_id_type=MESH,
        )

    def to_later(stage, m, act):
        if stage < last:
            act()
        else:
            pl.when(digit(stage) + m < stages[stage][1])(act)

    def from_earlier(stage, m, act):
        if stage < last:
            act()
        else:
            pl.when(digit(stage) - m >= 0)(act)

    def send_state(stage, g):
        st_send[stage, state_rows(g), :] = tot[state_rows(g), :].astype(BF16)
        for slot, m in slots[stage]:
            to_later(stage, m, lambda: state_copy(stage, slot, m, g).start())

    def take_state(stage, g):
        for slot, m in slots[stage]:
            def take():
                state_copy(stage, slot, m, g).wait_recv()
                got = st_recv[slot, state_rows(g), :].astype(F32)
                if stage < last:
                    tot[state_rows(g), :] += got
                    got = jnp.where(digit(stage) >= m, got, 0.0)
                pre[state_rows(g), :] += got

            from_earlier(stage, m, take)

    def head_cols(h):
        return pl.ds(h * HEAD_DIM, HEAD_DIM)

    loads[0].wait()
    loads[1].wait()

    def own_state(g):
        for h in range(g * group, (g + 1) * group):
            tot[head_cols(h), :] = lax.dot_general(
                kb[:, head_cols(h)], vb[:, head_cols(h)], (((0,), (0,)), ((), ())),
                preferred_element_type=F32,
            )

    own_state(0)
    pl.semaphore_wait(barrier, sum(map(len, slots)) + n_head - 1)
    for g in range(groups):
        if g > 0:
            own_state(g)
        if stages:
            send_state(0, g)
    pre[...] = jnp.zeros_like(pre)
    sq[...] = jnp.zeros_like(sq)
    loads[2].wait()
    loads[3].wait()

    def local(g):
        at = lax.broadcasted_iota(jnp.int32, (rows, rows), 0)
        of = lax.broadcasted_iota(jnp.int32, (rows, rows), 1)
        for h in range(g * group, (g + 1) * group):
            scores = lax.dot_general(
                qb[:, head_cols(h)], kb[:, head_cols(h)], (((1,), (1,)), ((), ())),
                preferred_element_type=F32,
            )
            scores = jnp.where(of <= at, scores, 0.0).astype(BF16)
            loc[:, head_cols(h)] = jnp.dot(
                scores, vb[:, head_cols(h)], preferred_element_type=F32
            )

    def z_copy(way, hop, c, origin):
        return pltpu.make_async_remote_copy(
            src_ref=yall.at[origin, c],
            dst_ref=yall.at[origin, c],
            send_sem=z_ssem.at[way, hop - 1, c],
            recv_sem=z_rsem.at[way, hop - 1, c],
            device_id={"head": me_h + 1 - 2 * way},
            device_id_type=MESH,
        )

    def finish(g):
        for number in range(group):
            h = g * group + number
            carried = jnp.dot(
                qb[:, head_cols(h)], pre[head_cols(h), :].astype(BF16),
                preferred_element_type=F32,
            )
            attended = (loc[:, head_cols(h)] + carried).astype(BF16).astype(F32)
            sq[...] += attended * attended
            gain = gain_ref[:, pl.ds(pl.multiple_of(me_h * width + h * HEAD_DIM, HEAD_DIM), HEAD_DIM)]
            gate = gb[:, head_cols(h)].astype(F32)
            yall[me_h, g, :, head_cols(number)] = (
                attended * gain * (1.0 / (1.0 + jnp.exp(-gate)))
            ).astype(BF16)

        @pl.when(me_h < n_head - 1)
        def _():
            z_copy(0, 1, g, me_h).start()

        @pl.when(me_h > 0)
        def _():
            z_copy(1, 1, g, me_h).start()

    for stage in range(last):
        for g in range(groups):
            take_state(stage, g)
            send_state(stage + 1, g)
    for load in w_loads:
        load.start()
    for g in range(groups):
        local(g)
    for g in range(groups):
        if stages:
            take_state(last, g)
        finish(g)

    def ms_copy(d, source):
        return pltpu.make_async_remote_copy(
            src_ref=ms.at[source],
            dst_ref=ms.at[source],
            send_sem=ms_ssem.at[d],
            recv_sem=ms_rsem.at[d],
            device_id={"head": lax.rem(me_h + d, n_head)},
            device_id_type=MESH,
        )

    row_total = jnp.sum(jnp.transpose(sq[...]), axis=0, keepdims=True)
    ms[me_h] = jnp.broadcast_to(row_total, ms.shape[1:])
    for d in range(1, n_head):
        ms_copy(d, me_h).start()
    acc[...] = jnp.zeros_like(acc)
    loads[4].wait()
    for load in w_loads:
        load.wait()

    def project(origin, c):
        at = pl.multiple_of(origin * width + c * group_width, group_width)
        acc[...] += jnp.dot(
            yall[origin, c], wb[pl.ds(at, group_width), :], preferred_element_type=F32
        )

    for d in range(1, n_head):
        def arrive(c, carry, d=d):
            @pl.when(me_h - d >= 0)
            def _():
                z_copy(0, d, c, me_h - d).wait_recv()

                @pl.when(me_h < n_head - 1)
                def _():
                    z_copy(0, d + 1, c, me_h - d).start()

            @pl.when(me_h + d < n_head)
            def _():
                z_copy(1, d, c, me_h + d).wait_recv()

                @pl.when(me_h > 0)
                def _():
                    z_copy(1, d + 1, c, me_h + d).start()

            if d == 1:
                project(me_h, c)

            @pl.when(me_h - d >= 0)
            def _():
                project(me_h - d, c)

            @pl.when(me_h + d < n_head)
            def _():
                project(me_h + d, c)

            return carry

        lax.fori_loop(0, groups, arrive, 0)

    for d in range(1, n_head):
        ms_copy(d, lax.rem(me_h + n_head - d, n_head)).wait_recv()
    total = ms[0, 0:1, :]
    for o in range(1, n_head):
        total = total + ms[o, 0:1, :]
    scale = lax.rsqrt(total / (n_head * width) + EPSILON)
    scale = jnp.transpose(jnp.broadcast_to(scale, (HEAD_DIM, rows)))
    for j in range(out_width // HEAD_DIM):
        out_ref[:, head_cols(j)] = (
            acc[:, head_cols(j)] * scale + rb[:, head_cols(j)].astype(F32)
        ).astype(out_ref.dtype)

    for stage in range(len(stages)):
        for slot, m in slots[stage]:
            for g in range(groups):
                to_later(stage, m, lambda: state_copy(stage, slot, m, g).wait_send())
    for d in range(1, n_head):
        ms_copy(d, me_h).wait_send()
        for c in range(groups):
            @pl.when(jnp.logical_and(me_h < n_head - 1, me_h - (d - 1) >= 0))
            def _(c=c, d=d):
                z_copy(0, d, c, me_h - (d - 1)).wait_send()

            @pl.when(jnp.logical_and(me_h > 0, me_h + (d - 1) < n_head))
            def _(c=c, d=d):
                z_copy(1, d, c, me_h + (d - 1)).wait_send()


def solution(mesh):
    n_ctx, n_head = mesh.shape["ctx"], mesh.shape["head"]
    steps = n_ctx.bit_length() - 1
    assert n_ctx == 2**steps
    stages = [(1, 2)] if steps % 2 else []
    for bit in range(steps % 2, steps, 2):
        stages.append((2**bit, 4))

    def on_device(queries, keys, values, gate_logits, norm_gain, out_weight, residual):
        rows, width = queries.shape
        inner, out_width = out_weight.shape
        heads = width // HEAD_DIM
        group = 2 if heads % 2 == 0 else 1
        groups = heads // group
        group_width = group * HEAD_DIM
        anywhere = pl.BlockSpec(memory_space=pl.ANY)
        vmem = pl.BlockSpec(memory_space=pltpu.VMEM)
        dma = pltpu.SemaphoreType.DMA
        hops = max(n_head - 1, 1)
        stage_count = max(len(stages), 1)
        slot_count = max(sum(radix - 1 for _, radix in stages), 1)
        return pl.pallas_call(
            functools.partial(kernel, tuple(stages), n_head, group),
            out_shape=jax.ShapeDtypeStruct((rows, out_width), residual.dtype),
            in_specs=[anywhere] * 4 + [vmem] + [anywhere] * 2,
            out_specs=vmem,
            scratch_shapes=[
                pltpu.VMEM((rows, width), BF16),
                pltpu.VMEM((rows, width), BF16),
                pltpu.VMEM((rows, width), BF16),
                pltpu.VMEM((rows, width), BF16),
                pltpu.VMEM((rows, out_width), BF16),
                pltpu.VMEM((inner, out_width), BF16),
                pltpu.VMEM((n_head, groups, rows, group_width), BF16),
                pltpu.VMEM((rows, out_width), F32),
                pltpu.VMEM((rows, width), F32),
                pltpu.VMEM((width, HEAD_DIM), F32),
                pltpu.VMEM((width, HEAD_DIM), F32),
                pltpu.VMEM((stage_count, width, HEAD_DIM), BF16),
                pltpu.VMEM((slot_count, width, HEAD_DIM), BF16),
                pltpu.VMEM((rows, HEAD_DIM), F32),
                pltpu.VMEM((n_head, 8, rows), F32),
                dma((5,)),
                dma((n_head,)),
                dma((slot_count, groups)),
                dma((slot_count, groups)),
                dma((2, hops, groups)),
                dma((2, hops, groups)),
                dma((n_head,)),
                dma((n_head,)),
            ],
            compiler_params=pltpu.CompilerParams(
                collective_id=0, has_side_effects=True, vmem_limit_bytes=62 * 1024 * 1024
            ),
        )(queries, keys, values, gate_logits, norm_gain[None, :], out_weight, residual)

    in_specs = (
        P("ctx", "head"),
        P("ctx", "head"),
        P("ctx", "head"),
        P("ctx", "head"),
        P(),
        P(None, "head"),
        P("ctx", "head"),
    )
    return jax.shard_map(
        on_device, mesh=mesh, in_specs=in_specs, out_specs=P("ctx", "head"), check_vma=False
    )
```
